256 devices in a mesh: group: 8 (over y, core), member: 32 (over z, x).
Axes of the slice: x: 4, y: 4, z: 8, core: 2. Of those that a mesh axis runs over, the one named last changes fastest.
Arguments:
- right_side: float32 [4096, 64, 128], P(('group', 'member')), may hold values from -70 to 70
- a_diagonal: float32 [4096, 128], P(('group', 'member')), may hold values from 1.05 to 3
- a_tiles: float32 [4096, 5, 128, 128], P(('group', 'member')), may hold values from 0 to 0.0333333333
- a_columns: int32 [4096, 5], P(('group', 'member')), may hold values from 0 to 23, as said below
- g_diagonal: float32 [4096, 128], P(('group', 'member')), may hold values from 0.5 to 2
- g_tiles: float32 [4096, 4, 128, 128], P(('group', 'member')), may hold values from 0 to 0.03125
- g_columns: int32 [4096, 4], P(('group', 'member')), may hold values from 0 to 23, as said below
- owned_counts: int32 [256], P(('group', 'member')), may hold values from 8 to 16, as said below
- send_lists: int32 [256, 4, 2], P(('group', 'member')), may hold values from 0 to 15, as said below
Outputs:
- solution: float32 [4096, 64, 128], P(('group', 'member'))
- residual: float32 [4096, 64, 128], P(('group', 'member'))
The draws below stay inside these ranges and needn't reach their ends.
Inputs may be any that keep to these rules, and one draw needn't show every extreme that they name: Block rows from owned_counts of a device up to 15 are padding; some device holds exactly 16 live block rows and some exactly 8. `send_lists`: the 8 entries of one device are distinct live block rows of that device; list j goes to the neighbour named in the reference program. `a_columns`: indices into the device's extended list; for a fixed tile position k no index appears twice among one device's block rows. `g_columns`: indices into the device's extended list; for a fixed tile position k no index appears twice among one device's block rows.
All inputs are finite; a program needn't handle non-finite values.
Results may differ from the reference program's by a relative error of at most 0.0003.
Values sent between devices are 32-bit elements; how exact they have to be, the bound alone decides.
No kernel may reach another device: no remote copies, remote signals or barrier semaphores. Data moves between devices by JAX's collectives and lax.ppermute only.
A program may use at most 64 MiB of HBM per device.

```python
import math
import jax
import jax.numpy as jnp
from jax import lax

BS = 128
W = 2
KA = 5
KG = 4
R = 16
NRHS = 64
ITERS = 3
S = 2
BLOCKS = 4096
N_GROUP = 8
N_MEMBER = 32


def device_counts(key):
    key = jax.random.fold_in(key, 11)
    devices = BLOCKS // R
    drawn = jax.random.randint(key, (devices,), R // 2, R + 1)
    ranked = jax.random.permutation(jax.random.fold_in(key, 1), devices)
    drawn = drawn.at[ranked[0]].set(R).at[ranked[1]].set(R // 2)
    return drawn.astype(jnp.int32)


def column_indices(key, tiles_per_row):
    devices = BLOCKS // R
    extent = R + 4 * S
    scores = jax.random.randint(key, (devices, tiles_per_row, extent), 0, 1 << 20) * extent + jnp.arange(extent)
    ranked = jnp.argsort(scores, axis=2)[:, :, :R]
    return jnp.transpose(ranked, (0, 2, 1)).reshape(BLOCKS, tiles_per_row).astype(jnp.int32)


def coupling_tiles(key, tiles_per_row, ceiling, low_end):

    def one_row(row_index):
        row_key = jax.random.fold_in(key, row_index)
        perm_key, value_key = jax.random.split(row_key)
        scores = jax.random.randint(perm_key, (tiles_per_row, BS), 0, 1 << 20) * BS + jnp.arange(BS)
        shifted = jnp.argsort(scores, axis=1)
        offset = (jnp.arange(BS)[None, None, :] - shifted[:, :, None]) % BS
        values = jax.random.uniform(value_key, (tiles_per_row, BS, BS), jnp.float32, low_end, 1.0)
        return jnp.where(offset < W, values * ceiling, 0.0).astype(jnp.float32)
    return lax.map(one_row, jnp.arange(BLOCKS))


def draw_owned_counts(key, part):
    return device_counts(key)


def draw_send_lists(key, part):
    counts = device_counts(key)
    key = jax.random.fold_in(key, 3)
    devices = BLOCKS // R
    positions = jnp.arange(R)[None, :]
    scores = jax.random.randint(key, (devices, R), 0, 1 << 20) * R + positions
    scores = scores + jnp.where(positions >= counts[:, None], 1 << 28, 0)
    ranked = jnp.argsort(scores, axis=1)
    return ranked[:, :4 * S].reshape(devices, 4, S).astype(jnp.int32)


def draw_a_columns(key, part):
    key = jax.random.fold_in(key, 5)
    return column_indices(key, KA)


def draw_g_columns(key, part):
    key = jax.random.fold_in(key, 7)
    return column_indices(key, KG)


def draw_a_tiles(key, part):
    key = jax.random.fold_in(key, 21)
    low_end = 0.0
    return coupling_tiles(key, KA, 1.0 / (3 * KA * W), low_end)


def draw_g_tiles(key, part):
    key = jax.random.fold_in(key, 23)
    low_end = 0.0
    return coupling_tiles(key, KG, 0.25 / (KG * W), low_end)


def draw_right_side(key, part):
    key = jax.random.fold_in(key, 31)
    scale_key, column_key, value_key = jax.random.split(key, 3)
    devices = BLOCKS // R
    position = jnp.arange(devices).astype(jnp.float32) / max(devices - 1, 1)
    block_scale = jnp.exp(jax.random.uniform(scale_key, (BLOCKS,), jnp.float32, -0.8, 0.8))
    column_scale = jnp.exp(jax.random.uniform(column_key, (NRHS,), jnp.float32, -0.8, 0.8))
    device_ramp = 1.0 + 2.0 * position
    values = jax.random.truncated_normal(value_key, -4.0, 4.0, (BLOCKS, NRHS, BS), jnp.float32)
    row_scale = jnp.repeat(device_ramp, R) * block_scale
    return (values * row_scale[:, None, None] * column_scale[None, :, None]).astype(jnp.float32)


def block_levels(stream_key, dims, shards, low, largest):
    level, own = 1.0, jax.random.fold_in(stream_key, 6)
    for dim, shards_of in shards:
        steps = jnp.exp(jax.random.uniform(jax.random.fold_in(own, dim), (shards_of,), jnp.float32, low / len(shards), largest / len(shards)))
        level = level * jnp.repeat(steps, dims[dim] // shards_of).reshape([-1 if axis == dim else 1 for axis in range(len(dims))])
    return level


def setup_inputs(seed: int = 0) -> dict:
    key_of = jax.random.split(jax.random.key(seed), 10)
    right_side = draw_right_side(jax.random.fold_in(key_of[9], 71), 0)
    a_diagonal = jnp.clip(jnp.exp(math.log(3.0) - 1.0498222 * jax.random.uniform(key_of[1], (BLOCKS, BS), jnp.float32) ** block_levels(key_of[1], (BLOCKS, BS), ((0, 256),), -0.2, 0.2)), 1.05, 3.0)
    a_tiles = draw_a_tiles(jax.random.fold_in(key_of[9], 71), 0)
    a_columns = draw_a_columns(jax.random.fold_in(key_of[9], 71), 0)
    g_diagonal = jnp.clip(jnp.exp(math.log(2.0) - 1.3862944 * jax.random.uniform(key_of[4], (BLOCKS, BS), jnp.float32) ** block_levels(key_of[4], (BLOCKS, BS), ((0, 256),), -0.2, 0.2)), 0.5, 2.0)
    g_tiles = draw_g_tiles(jax.random.fold_in(key_of[9], 71), 0)
    g_columns = draw_g_columns(jax.random.fold_in(key_of[9], 71), 0)
    owned_counts = draw_owned_counts(jax.random.fold_in(key_of[9], 71), 0)
    send_lists = draw_send_lists(jax.random.fold_in(key_of[9], 71), 0)
    return dict(right_side=right_side, a_diagonal=a_diagonal, a_tiles=a_tiles, a_columns=a_columns, g_diagonal=g_diagonal, g_tiles=g_tiles, g_columns=g_columns, owned_counts=owned_counts, send_lists=send_lists)


PRECISE = lax.Precision.HIGHEST


def neighbour_slots(vector, outgoing):
    packed = jax.vmap(jax.vmap(lambda block_set, chosen: jnp.take(block_set, chosen, axis=0)))(vector, outgoing)
    member_zero = jnp.zeros_like(packed[:, :1, 0])
    group_zero = jnp.zeros_like(packed[:1, :, 0])
    below_member = jnp.concatenate([member_zero, packed[:, :-1, 0]], axis=1)
    above_member = jnp.concatenate([packed[:, 1:, 1], member_zero], axis=1)
    below_group = jnp.concatenate([group_zero, packed[:-1, :, 2]], axis=0)
    above_group = jnp.concatenate([packed[1:, :, 3], group_zero], axis=0)
    return jnp.concatenate([vector, below_member, above_member, below_group, above_group], axis=2)


def device_rows(tile_set, column_ids, extended):
    picked = jnp.take(extended, column_ids.reshape(-1), axis=0)
    picked = picked.reshape(column_ids.shape + extended.shape[1:])
    return jnp.einsum('rkij,rknj->rni', tile_set, picked, precision=PRECISE)


def row_products(tile_set, column_ids, extended):
    return lax.map(lambda group_part: jax.vmap(device_rows)(*group_part), (tile_set, column_ids, extended))


def device_columns(tile_set, column_ids, vector):
    contrib = jnp.einsum('rkij,rni->rknj', tile_set, vector, precision=PRECISE)
    flattened = contrib.reshape((-1,) + vector.shape[1:])
    empty = jnp.zeros((R + 4 * S,) + vector.shape[1:], jnp.float32)
    return empty.at[column_ids.reshape(-1)].add(flattened)


def add_back(own_block, chosen, incoming):
    return own_block.at[chosen.reshape(-1)].add(incoming.reshape((-1,) + incoming.shape[2:]))


def column_sums(tile_set, column_ids, vector, outgoing):
    sums_wide = lax.map(lambda group_part: jax.vmap(device_columns)(*group_part), (tile_set, column_ids, vector))
    own_rows = sums_wide[:, :, :R]
    pieces = [sums_wide[:, :, R + facing * S:R + (facing + 1) * S] for facing in range(4)]
    member_zero = jnp.zeros_like(pieces[0][:, :1])
    group_zero = jnp.zeros_like(pieces[0][:1])
    arrivals = jnp.stack([
        jnp.concatenate([pieces[0][:, 1:], member_zero], axis=1),
        jnp.concatenate([member_zero, pieces[1][:, :-1]], axis=1),
        jnp.concatenate([pieces[2][1:], group_zero], axis=0),
        jnp.concatenate([group_zero, pieces[3][:-1]], axis=0)], axis=2)
    return jax.vmap(jax.vmap(add_back))(own_rows, outgoing, arrivals)


def reference(right_side, a_diagonal, a_tiles, a_columns, g_diagonal, g_tiles, g_columns, owned_counts, send_lists):
    device_grid = (N_GROUP, N_MEMBER)

    def split_devices(values):
        return values.reshape(device_grid + (R,) + values.shape[1:])

    live_rows = jnp.arange(R, dtype=jnp.int32)[None, None, :] < owned_counts.reshape(device_grid)[:, :, None]
    live_rows = live_rows.astype(jnp.float32)[:, :, :, None, None]
    outgoing = send_lists.reshape(device_grid + (4, S))
    a_scale = split_devices(a_diagonal)[:, :, :, None, :]
    g_scale = split_devices(g_diagonal)[:, :, :, None, :]
    a_set, a_ids = split_devices(a_tiles), split_devices(a_columns)
    g_set, g_ids = split_devices(g_tiles), split_devices(g_columns)

    def apply_pressure(vector):
        lower_part = row_products(a_set, a_ids, neighbour_slots(vector, outgoing))
        upper_part = column_sums(a_set, a_ids, vector, outgoing)
        return (a_scale * vector - lower_part - upper_part) * live_rows

    def apply_factors(vector):
        halfway = (g_scale * vector + row_products(g_set, g_ids, neighbour_slots(vector, outgoing))) * live_rows
        return (g_scale * halfway + column_sums(g_set, g_ids, halfway, outgoing)) * live_rows

    def inner(first_vec, second_vec):
        return jnp.sum(first_vec * second_vec, axis=(0, 1, 2, 4))

    residual = split_devices(right_side) * live_rows
    solution = jnp.zeros_like(residual)
    preconditioned = apply_factors(residual)
    rho_now = inner(residual, preconditioned)
    direction = preconditioned
    for iteration in range(ITERS):
        pressure_image = apply_pressure(direction)
        step_size = rho_now / inner(direction, pressure_image)
        solution = solution + step_size[:, None] * direction
        residual = residual - step_size[:, None] * pressure_image
        if iteration + 1 < ITERS:
            preconditioned = apply_factors(residual)
            rho_next = inner(residual, preconditioned)
            direction = preconditioned + (rho_next / rho_now)[:, None] * direction
            rho_now = rho_next
    return solution.reshape(right_side.shape), residual.reshape(right_side.shape)
```

```python
import functools

import jax
import jax.numpy as jnp
from jax import lax
from jax.experimental import pallas as pl
from jax.experimental.pallas import tpu as pltpu
from jax.sharding import PartitionSpec as P

SHIFT = 4.0
LISTS = 4
f32 = jnp.float32
bf16 = jnp.bfloat16
VMEM = pl.BlockSpec(memory_space=pltpu.VMEM)
SMEM = pl.BlockSpec(memory_space=pltpu.SMEM)


def halves(x):
    high = x.astype(bf16)
    low = (x - high.astype(f32)).astype(bf16)
    return high, low


def stacked(x):
    return jnp.concatenate(halves(x), axis=0)


def beside(x):
    return jnp.concatenate(halves(x), axis=1)


def product(rows, tile):
    out = jnp.dot(rows, tile, preferred_element_type=f32)
    n, m = out.shape[0] // 2, out.shape[1] // 2
    out = out[:n] + out[n:]
    return out[:, :m] + out[:, m:]


class Meta:
    def __init__(self, ref, tiles):
        self.ref = ref
        self.tiles = tiles

    def column(self, b, k):
        return self.ref[b * self.tiles + k]

    def sent(self, i, s):
        return self.ref[16 * self.tiles + 2 * i + s]

    def live(self, b):
        return b < self.ref[16 * self.tiles + 8]

    def valid(self, i):
        return self.ref[16 * self.tiles + 9 + i] > 0


def assemble(meta, part, msgs, recvs, ext):
    for b in range(16):
        ext[b] = part[b]
    for i in range(LISTS):
        valid = meta.valid(i)
        for s in range(2):
            row = meta.sent(i ^ 1, s)
            ext[row] += jnp.where(valid, recvs[i][2 + s], 0.0)
            ext[16 + 2 * i + s] = jnp.where(valid, recvs[i][s] + msgs[i ^ 1][2 + s], 0.0)


def fill_messages(meta, part, sums, sign, msgs):
    for i in range(LISTS):
        for s in range(2):
            msgs[i][s] = part[meta.sent(i, s)]
            msgs[i][2 + s] = sign * sums[16 + 2 * (i ^ 1) + s]


def forward_row(meta, b, tile_ref, split_ref):
    picked = []
    turned = []
    for k in range(meta.tiles):
        picked.append(split_ref[meta.column(b, k)])
        turned.append(beside(tile_ref[b, k].T))
    return product(jnp.concatenate(picked, axis=1), jnp.concatenate(turned, axis=0))


def transposed_row(meta, b, tile_ref, rows, sums):
    for k in range(meta.tiles):
        sums[meta.column(b, k)] += product(rows, beside(tile_ref[b, k]))


def pack_kernel(meta_ref, right_ref, m0, m1, m2, m3):
    meta = Meta(meta_ref, 4)
    for i, msg in enumerate((m0, m1, m2, m3)):
        for s in range(2):
            msg[s] = right_ref[meta.sent(i, s)]


def factor_kernel(first, meta_ref, diag_ref, tile_ref, *refs):
    meta = Meta(meta_ref, 4)
    if first:
        right_ref, r0, r1, r2, r3 = refs[:5]
        recvs = (r0, r1, r2, r3)
        own_ref, half_ref, part_ref, m0, m1, m2, m3, ext, split_ref, sums = refs[5:]
        for b in range(16):
            ext[b] = jnp.where(meta.live(b), right_ref[b], 0.0)
        for i in range(LISTS):
            for s in range(2):
                ext[16 + 2 * i + s] = jnp.where(meta.valid(i), recvs[i][s], 0.0)
    else:
        part_in = refs[0]
        own_ref, half_ref, part_ref, m0, m1, m2, m3, ext, split_ref, sums = refs[9:]
        assemble(meta, part_in, refs[1:5], refs[5:9], ext)
    for m in range(24):
        split_ref[m] = stacked(ext[m])
    sums[...] = jnp.zeros_like(sums)
    for b in range(16):
        own_ref[b] = ext[b]
    for b in range(16):
        forward = forward_row(meta, b, tile_ref, split_ref)
        half = jnp.where(meta.live(b), diag_ref[b : b + 1] * ext[b] + forward, 0.0)
        half_ref[b] = half
        transposed_row(meta, b, tile_ref, stacked(half), sums)
    for b in range(16):
        part_ref[b] = jnp.where(meta.live(b), diag_ref[b : b + 1] * half_ref[b] + sums[b], 0.0)
    fill_messages(meta, part_ref, sums, 1.0, (m0, m1, m2, m3))


def pressure_kernel(last, meta_ref, diag_ref, tile_ref, *refs):
    meta = Meta(meta_ref, 5)
    part_in, msgs, recvs = refs[0], refs[1:5], refs[5:9]
    if last:
        gram_ref = refs[9]
        own_ref, part_ref, m0, m1, m2, m3, pay_ref, ext, split_ref, sums = refs[10:]
    else:
        basis_ref = refs[9]
        own_ref, part_ref, m0, m1, m2, m3, ext, split_ref, sums = refs[10:]
    assemble(meta, part_in, msgs, recvs, ext)
    for m in range(24):
        split_ref[m] = stacked(ext[m])
    sums[...] = jnp.zeros_like(sums)
    for b in range(16):
        own_ref[b] = ext[b]
    energy = jnp.zeros(ext.shape[1:], f32)
    for b in range(16):
        forward = forward_row(meta, b, tile_ref, split_ref)
        scaled = diag_ref[b : b + 1] * ext[b]
        part_ref[b] = scaled - forward
        if last:
            energy = energy + ext[b] * (scaled - 2.0 * forward)
        transposed_row(meta, b, tile_ref, split_ref[b], sums)
    for b in range(16):
        value = part_ref[b] - sums[b]
        if not last:
            value = value - SHIFT * basis_ref[b]
        part_ref[b] = jnp.where(meta.live(b), value, 0.0)
    fill_messages(meta, part_ref, sums, -1.0, (m0, m1, m2, m3))
    if last:
        place = lax.broadcasted_iota(jnp.int32, energy.shape, 1)
        table = gram_ref[...] + jnp.where(place == 6, jnp.sum(energy, axis=1, keepdims=True), 0.0)
        turned = jnp.concatenate([table, jnp.zeros_like(table)], axis=0).T[:8]
        for i in range(8):
            pay_ref[i] = turned


def gram_kernel(y0, y1, y2, out_ref):
    pairs = ((y0, y0), (y0, y1), (y0, y2), (y1, y1), (y1, y2), (y2, y2))
    totals = [jnp.zeros(out_ref.shape, f32) for _ in pairs]
    for b in range(16):
        totals = [total + left[b] * right[b] for total, (left, right) in zip(totals, pairs)]
    place = lax.broadcasted_iota(jnp.int32, out_ref.shape, 1)
    table = jnp.zeros(out_ref.shape, f32)
    for i, total in enumerate(totals):
        table = table + jnp.where(place == i, jnp.sum(total, axis=1, keepdims=True), 0.0)
    out_ref[...] = table


def cg_scalars(g):
    gram = {(0, 0): g[0], (0, 1): g[1], (0, 2): g[2], (1, 1): g[3], (1, 2): g[4], (2, 2): g[5]}
    energy = {(2, 2): g[6]}
    for i in range(2):
        for j in range(i, 3):
            energy[i, j] = gram[min(i + 1, j), max(i + 1, j)] + SHIFT * gram[i, j]

    def form(table, c):
        total = 0.0
        for i in range(len(c)):
            for j in range(i, len(c)):
                term = c[i] * c[j] * table[i, j]
                total = total + (term if i == j else 2.0 * term)
        return total

    zero = jnp.zeros_like(g[0])
    one = jnp.ones_like(g[0])
    x = [zero, zero, zero]
    r = [one, zero, zero, zero]
    p = [one]
    rho = gram[0, 0]
    for step in range(3):
        alpha = rho / form(energy, p)
        for i, c in enumerate(p):
            x[i] = x[i] + alpha * c
            r[i] = r[i] - SHIFT * (alpha * c)
            r[i + 1] = r[i + 1] - alpha * c
        if step < 2:
            rho_next = form(gram, r[: step + 2])
            beta = rho_next / rho
            p = [r[i] + beta * (p[i] if i < len(p) else 0.0) for i in range(step + 2)]
            rho = rho_next
    return x + r


def final_kernel(meta_ref, sums_ref, v0, v1, v2, w0, w1, w2, part_ref, r0, r1, r2, r3, x_ref, res_ref, w3):
    meta = Meta(meta_ref, 5)
    total = sums_ref[0]
    for i in range(1, sums_ref.shape[0]):
        total = total + sums_ref[i]
    rows = cg_scalars([total[i : i + 1] for i in range(7)])
    rows = jnp.concatenate(rows + [jnp.zeros((121, 128), f32)], axis=0)
    columns = rows.T[:64]
    c = [jnp.broadcast_to(columns[:, i : i + 1], (64, 128)) for i in range(7)]
    for b in range(16):
        w3[b] = part_ref[b]
    for i, recv in enumerate((r0, r1, r2, r3)):
        for s in range(2):
            w3[meta.sent(i ^ 1, s)] += jnp.where(meta.valid(i), recv[2 + s], 0.0)
    for b in range(16):
        x_ref[b] = c[0] * v0[b] + c[1] * v1[b] + c[2] * v2[b]
        res_ref[b] = c[3] * w0[b] + c[4] * w1[b] + (c[5] - SHIFT * c[6]) * w2[b] + c[6] * w3[b]


def call(kernel, outs, scratch=(), smem=1):
    def run(*args):
        return pl.pallas_call(
            kernel,
            out_shape=tuple(jax.ShapeDtypeStruct(shape, f32) for shape in outs),
            in_specs=[SMEM] * smem + [VMEM] * (len(args) - smem),
            out_specs=(VMEM,) * len(outs),
            scratch_shapes=list(scratch),
            compiler_params=pltpu.CompilerParams(vmem_limit_bytes=32 * 2**20),
        )(*args)

    return run


def on_device(
    right_side,
    a_diagonal,
    a_tiles,
    a_columns,
    g_diagonal,
    g_tiles,
    g_columns,
    owned_counts,
    send_lists,
):
    groups, members = lax.axis_size("group"), lax.axis_size("member")
    group, member = lax.axis_index("group"), lax.axis_index("member")
    valid = jnp.stack([member > 0, member < members - 1, group > 0, group < groups - 1])
    tail = [send_lists.reshape(-1), owned_counts, valid.astype(jnp.int32)]
    a_meta = jnp.concatenate([a_columns.reshape(-1)] + tail)
    g_meta = jnp.concatenate([g_columns.reshape(-1)] + tail)

    own = (16, 64, 128)
    message = (4, 64, 128)

    def exchange(msgs):
        out = []
        for msg, axis, size, way in zip(
            msgs, ("member", "member", "group", "group"), (members, members, groups, groups), (1, -1, 1, -1)
        ):
            out.append(lax.ppermute(msg, axis, [(i, (i + way) % size) for i in range(size)]))
        return out

    scratch = [pltpu.VMEM((24, 64, 128), f32), pltpu.VMEM((24, 128, 128), bf16), pltpu.VMEM((24, 64, 128), f32)]
    msgs = call(pack_kernel, [(2, 64, 128)] * 4)(g_meta, right_side)
    recvs = exchange(msgs)
    basis_w, basis_v, halves_y = [], [], []
    for k in range(3):
        if k == 0:
            operands = (right_side, *recvs)
        else:
            operands = (part, *msgs, *recvs)
        w, y, part, *msgs = call(functools.partial(factor_kernel, k == 0), [own] * 3 + [message] * 4, scratch)(
            g_meta, g_diagonal, g_tiles, *operands
        )
        recvs = exchange(msgs)
        basis_w.append(w)
        halves_y.append(y)
        if k < 2:
            extra = w
            outs = [own, own] + [message] * 4
        else:
            (extra,) = call(gram_kernel, [(64, 128)], smem=0)(*halves_y)
            outs = [own, own] + [message] * 4 + [(groups, 8, 128)]
        v, part, *msgs = call(functools.partial(pressure_kernel, k == 2), outs, scratch)(
            a_meta, a_diagonal, a_tiles, part, *msgs, *recvs, extra
        )
        basis_v.append(v)
        if k == 2:
            *msgs, payload = msgs
        recvs = exchange(msgs)
    sums = jnp.sum(lax.all_to_all(payload, "group", 0, 0), axis=0)
    sums = lax.all_to_all(jnp.broadcast_to(sums[None], (members, 8, 128)), "member", 0, 0)
    return call(final_kernel, [own, own], [pltpu.VMEM(own, f32)])(
        a_meta, sums, *basis_v, *basis_w, part, *recvs
    )


def solution(mesh):
    return jax.shard_map(
        on_device,
        mesh=mesh,
        in_specs=(
            P(("group", "member"), None, None),
            P(("group", "member"), None),
            P(("group", "member"), None, None, None),
            P(("group", "member"), None),
            P(("group", "member"), None),
            P(("group", "member"), None, None, None),
            P(("group", "member"), None),
            P(("group", "member")),
            P(("group", "member"), None, None),
        ),
        out_specs=(P(("group", "member"), None, None), P(("group", "member"), None, None)),
        check_vma=False,
    )
```

```python
import functools

import jax
import jax.numpy as jnp
from jax import lax
from jax.experimental import pallas as pl
from jax.experimental.pallas import tpu as pltpu
from jax.sharding import PartitionSpec as P

SHIFT = 4.0
LISTS = 4
VMEM_LIMIT = 10 * 2**20
CANCELLATION = 100.0
ITERS = 3
PRECISE = lax.Precision.HIGHEST
f32 = jnp.float32
bf16 = jnp.bfloat16
VMEM = pl.BlockSpec(memory_space=pltpu.VMEM)
HBM = pl.BlockSpec(memory_space=pltpu.HBM)
SMEM = pl.BlockSpec(memory_space=pltpu.SMEM)


def halves(x):
    high = x.astype(bf16)
    low = (x - high.astype(f32)).astype(bf16)
    return high, low


def stacked(x):
    return jnp.concatenate(halves(x), axis=0)


def beside(x):
    return jnp.concatenate(halves(x), axis=1)


def product(rows, tile):
    out = jnp.dot(rows, tile, preferred_element_type=f32)
    n, m = out.shape[0] // 2, out.shape[1] // 2
    out = out[:n] + out[n:]
    return out[:, :m] + out[:, m:]


class Meta:
    def __init__(self, ref, tiles):
        self.ref = ref
        self.tiles = tiles
        self.base = 16 * tiles

    def column(self, b, k):
        return self.ref[b * self.tiles + k]

    def listed(self, c, s):
        return self.ref[self.base + 2 * c + s]

    def slot(self, c, s):
        return self.ref[self.base + 8 + c] + s

    def valid(self, c):
        return self.ref[self.base + 12 + c] > 0

    def live(self, b):
        return b < self.ref[self.base + 16]


def assemble(meta, part, msgs, recvs, ext):
    for b in range(16):
        ext[b] = part[b]
    for c in range(LISTS):
        valid = meta.valid(c)
        for s in range(2):
            ext[meta.listed(c, s)] += jnp.where(valid, recvs[c][2 + s], 0.0)
            ext[meta.slot(c, s)] = jnp.where(valid, recvs[c][s] + msgs[c][2 + s], 0.0)


def fill_messages(meta, part, sums, sign, msgs):
    for c in range(LISTS):
        for s in range(2):
            msgs[c][s] = part[meta.listed(c, s)]
            msgs[c][2 + s] = sign * sums[meta.slot(c, s)]


def forward_row(meta, b, turned_ref, split_ref):
    picked = [split_ref[meta.column(b, k)] for k in range(meta.tiles)]
    return product(jnp.concatenate(picked, axis=1), turned_ref[b])


def transposed_row(meta, b, near_ref, rows, sums):
    for k in range(meta.tiles):
        sums[meta.column(b, k)] += product(rows, near_ref[b, k])


def prepare_tiles(hbm, near, turned, buffer, sems):
    copies = [pltpu.make_async_copy(hbm.at[b], buffer.at[b], sems.at[b]) for b in range(16)]
    for copy in copies:
        copy.start()
    for b in range(16):
        copies[b].wait()
        for k in range(hbm.shape[1]):
            tile = buffer[b, k]
            near[b, k] = beside(tile)
            turned[b, 128 * k : 128 * (k + 1)] = beside(tile.T)


def ways_of(sizes):
    ways = []
    for axis, size in sizes:
        place = lax.axis_index(axis)
        odd = place % 2
        ways.append((1 - odd, jnp.where(odd == 1, place < size - 1, place > 0)))
        ways.append((odd, jnp.where(odd == 1, place > 0, place < size - 1)))
    return ways


def pack_kernel(sizes, lists_hbm, right_hbm, m0, m1, m2, m3, lists, sem, block_sems):
    load = pltpu.make_async_copy(lists_hbm, lists, sem)
    load.start()
    load.wait()
    copies = []
    for c, ((down, _), msg) in enumerate(zip(ways_of(sizes), (m0, m1, m2, m3))):
        for s in range(2):
            row = lists[0, 2 * (c // 2) + down, s]
            copies.append(pltpu.make_async_copy(right_hbm.at[row], msg.at[s], block_sems.at[2 * c + s]))
    for copy in copies:
        copy.start()
    for copy in copies:
        copy.wait()


def setup_kernel(sizes, a_hbm, g_hbm, count_hbm, lists_hbm, a_meta, g_meta, *scratch):
    a_cols, g_cols, count, lists, sems = scratch
    loads = []
    for i, (source, here) in enumerate(((a_hbm, a_cols), (g_hbm, g_cols), (count_hbm, count), (lists_hbm, lists))):
        loads.append(pltpu.make_async_copy(source, here, sems.at[i]))
        loads[-1].start()
    for load in loads:
        load.wait()
    for cols, meta, tiles in ((a_cols, a_meta, 5), (g_cols, g_meta, 4)):
        base = 16 * tiles
        for b in range(16):
            for k in range(tiles):
                meta[b * tiles + k] = cols[b, k]
        for c, (down, exists) in enumerate(ways_of(sizes)):
            first = 2 * (c // 2)
            for s in range(2):
                meta[base + 2 * c + s] = lists[0, first + down, s]
            meta[base + 8 + c] = 16 + 2 * (first + 1 - down)
            meta[base + 12 + c] = exists.astype(jnp.int32)
        meta[base + 16] = count[0]


def factor_kernel(first, meta_ref, diag_ref, near_ref, turned_ref, *refs):
    meta = Meta(meta_ref, 4)
    if first:
        right_ref, r0, r1, r2, r3 = refs[:5]
        recvs = (r0, r1, r2, r3)
        own_ref, half_ref, part_ref, m0, m1, m2, m3, ext, split_ref, sums, half_split = refs[5:]
        for b in range(16):
            ext[b] = jnp.where(meta.live(b), right_ref[b], 0.0)
        for c in range(LISTS):
            for s in range(2):
                ext[meta.slot(c, s)] = jnp.where(meta.valid(c), recvs[c][s], 0.0)
    else:
        part_in = refs[0]
        own_ref, half_ref, part_ref, m0, m1, m2, m3, ext, split_ref, sums, half_split = refs[9:]
        assemble(meta, part_in, refs[1:5], refs[5:9], ext)
    for m in range(24):
        split_ref[m] = stacked(ext[m])
    sums[...] = jnp.zeros_like(sums)
    for b in range(16):
        own_ref[b] = ext[b]
    for b in range(16):
        forward = forward_row(meta, b, turned_ref, split_ref)
        half = jnp.where(meta.live(b), diag_ref[b : b + 1] * ext[b] + forward, 0.0)
        half_ref[b] = half
        half_split[b] = stacked(half)
    for b in range(16):
        transposed_row(meta, b, near_ref, half_split[b], sums)
    for b in range(16):
        part_ref[b] = jnp.where(meta.live(b), diag_ref[b : b + 1] * half_ref[b] + sums[b], 0.0)
    fill_messages(meta, part_ref, sums, 1.0, (m0, m1, m2, m3))


def pressure_kernel(last, meta_ref, diag_ref, near_ref, turned_ref, *refs):
    meta = Meta(meta_ref, 5)
    part_in, msgs, recvs = refs[0], refs[1:5], refs[5:9]
    if last:
        gram_ref = refs[9]
        own_ref, part_ref, m0, m1, m2, m3, pay_ref, ext, split_ref, sums = refs[10:]
    else:
        basis_ref = refs[9]
        own_ref, part_ref, m0, m1, m2, m3, ext, split_ref, sums = refs[10:]
    assemble(meta, part_in, msgs, recvs, ext)
    for m in range(24):
        split_ref[m] = stacked(ext[m])
    sums[...] = jnp.zeros_like(sums)
    for b in range(16):
        own_ref[b] = ext[b]
    energy = jnp.zeros(ext.shape[1:], f32)
    for b in range(16):
        forward = forward_row(meta, b, turned_ref, split_ref)
        scaled = diag_ref[b : b + 1] * ext[b]
        part_ref[b] = scaled - forward
        if last:
            energy = energy + ext[b] * (scaled - 2.0 * forward)
        transposed_row(meta, b, near_ref, split_ref[b], sums)
    for b in range(16):
        value = part_ref[b] - sums[b]
        if not last:
            value = value - SHIFT * basis_ref[b]
        part_ref[b] = jnp.where(meta.live(b), value, 0.0)
    if not last:
        fill_messages(meta, part_ref, sums, -1.0, (m0, m1, m2, m3))
    else:
        for c, msg in enumerate((m0, m1, m2, m3)):
            for s in range(2):
                msg[s] = -sums[meta.slot(c, s)]
        place = lax.broadcasted_iota(jnp.int32, energy.shape, 1)
        table = gram_ref[...] + jnp.where(place == 6, jnp.sum(energy, axis=1, keepdims=True), 0.0)
        turned = jnp.concatenate([table, jnp.zeros_like(table)], axis=0).T[:8]
        for i in range(8):
            pay_ref[i] = turned


def gram_kernel(y0, y1, y2, out_ref):
    pairs = ((y0, y0), (y0, y1), (y0, y2), (y1, y1), (y1, y2), (y2, y2))
    totals = [jnp.zeros(out_ref.shape, f32) for _ in pairs]
    for b in range(16):
        totals = [total + left[b] * right[b] for total, (left, right) in zip(totals, pairs)]
    place = lax.broadcasted_iota(jnp.int32, out_ref.shape, 1)
    table = jnp.zeros(out_ref.shape, f32)
    for i, total in enumerate(totals):
        table = table + jnp.where(place == i, jnp.sum(total, axis=1, keepdims=True), 0.0)
    out_ref[...] = table


def cg_scalars(g):
    gram = {(0, 0): g[0], (0, 1): g[1], (0, 2): g[2], (1, 1): g[3], (1, 2): g[4], (2, 2): g[5]}
    size = {at: jnp.abs(value) for at, value in gram.items()}
    energy = {(2, 2): g[6]}
    energy_size = {(2, 2): jnp.abs(g[6])}
    for i in range(2):
        for j in range(i, 3):
            at = (min(i + 1, j), max(i + 1, j))
            energy[i, j] = gram[at] + SHIFT * gram[i, j]
            energy_size[i, j] = size[at] + SHIFT * size[i, j]
    lost = jnp.zeros_like(g[0])

    def form(table, sizes, c, lost):
        total, scale = 0.0, 0.0
        for i in range(len(c)):
            for j in range(i, len(c)):
                pair = c[i] * c[j] * (1.0 if i == j else 2.0)
                total = total + pair * table[i, j]
                scale = scale + jnp.abs(pair) * sizes[i, j]
        return total, jnp.maximum(lost, scale - CANCELLATION * total)

    zero = jnp.zeros_like(g[0])
    one = jnp.ones_like(g[0])
    x = [zero, zero, zero]
    r = [one, zero, zero, zero]
    p = [one]
    rho = gram[0, 0]
    for step in range(ITERS):
        image, lost = form(energy, energy_size, p, lost)
        alpha = rho / image
        for i, c in enumerate(p):
            x[i] = x[i] + alpha * c
            r[i] = r[i] - SHIFT * (alpha * c)
            r[i + 1] = r[i + 1] - alpha * c
        if step + 1 < ITERS:
            rho_next, lost = form(gram, size, r[: step + 2], lost)
            beta = rho_next / rho
            p = [r[i] + beta * (p[i] if i < len(p) else 0.0) for i in range(step + 2)]
            rho = rho_next
    return x + r, lost


def scalar_kernel(sums_ref, table_ref, flag_ref):
    total = sums_ref[0]
    for i in range(1, sums_ref.shape[0]):
        total = total + sums_ref[i]
    rows, lost = cg_scalars([total[i : i + 1] for i in range(7)])
    lane = lax.broadcasted_iota(jnp.int32, lost.shape, 1)
    fine = jnp.where((lost <= 0.0) | (lane >= 64), 0.0, 1.0)
    flag_ref[0] = (jnp.max(fine) > 0.0).astype(jnp.int32)
    rows = jnp.concatenate(rows + [jnp.zeros((121, 128), f32)], axis=0)
    table_ref[...] = rows.T[:64]


def final_kernel(meta_ref, table_ref, v0, v1, v2, w0, w1, w2, part_ref, r0, r1, r2, r3, x_ref, res_ref, w3):
    meta = Meta(meta_ref, 5)
    c = [jnp.broadcast_to(table_ref[:, i : i + 1], (64, 128)) for i in range(7)]
    for b in range(16):
        w3[b] = part_ref[b]
    for i, recv in enumerate((r0, r1, r2, r3)):
        for s in range(2):
            w3[meta.listed(i, s)] += jnp.where(meta.valid(i), recv[s], 0.0)
    for b in range(16):
        x_ref[b] = c[0] * v0[b] + c[1] * v1[b] + c[2] * v2[b]
        res_ref[b] = c[3] * w0[b] + c[4] * w1[b] + (c[5] - SHIFT * c[6]) * w2[b] + c[6] * w3[b]


def plain_steps(
    right_side, a_diagonal, a_tiles, a_columns, g_diagonal, g_tiles, g_columns, owned_counts, send_lists
):
    outgoing = send_lists[0]
    live = (jnp.arange(16) < owned_counts[0]).astype(f32)[:, None, None]
    a_scale, g_scale = a_diagonal[:, None, :], g_diagonal[:, None, :]
    steps = (("member", 1), ("member", -1), ("group", 1), ("group", -1))

    def move(block, axis, way):
        size = lax.axis_size(axis)
        return lax.ppermute(block, axis, [(i, i + way) for i in range(size) if 0 <= i + way < size])

    def forward(tiles, columns, vector):
        halo = [move(vector[outgoing[j]], axis, way) for j, (axis, way) in enumerate(steps)]
        picked = jnp.concatenate([vector] + halo, axis=0)[columns]
        return jnp.einsum("rkij,rknj->rni", tiles, picked, precision=PRECISE)

    def backward(tiles, columns, vector):
        parts = jnp.einsum("rkij,rni->rknj", tiles, vector, precision=PRECISE)
        onehot = (columns.reshape(-1)[:, None] == jnp.arange(24)[None, :]).astype(f32)
        wide = jnp.einsum("te,tnb->enb", onehot, parts.reshape((-1,) + vector.shape[1:]), precision=PRECISE)
        back = [move(wide[16 + 2 * j : 18 + 2 * j], axis, -way) for j, (axis, way) in enumerate(steps)]
        places = (outgoing.reshape(-1)[:, None] == jnp.arange(16)[None, :]).astype(f32)
        return wide[:16] + jnp.einsum("sr,snb->rnb", places, jnp.concatenate(back, axis=0), precision=PRECISE)

    def factors(vector):
        half = (g_scale * vector + forward(g_tiles, g_columns, vector)) * live
        return (g_scale * half + backward(g_tiles, g_columns, half)) * live

    def inner(u, w):
        return lax.psum(jnp.sum(u * w, axis=(0, 2)), ("group", "member"))

    def body(_, carry):
        x, res, direction, rho = carry
        low = forward(a_tiles, a_columns, direction)
        image = (a_scale * direction - low - backward(a_tiles, a_columns, direction)) * live
        alpha = (rho / inner(direction, image))[:, None]
        x = x + alpha * direction
        res = res - alpha * image
        z = factors(res)
        rho_next = inner(res, z)
        return x, res, z + (rho_next / rho)[:, None] * direction, rho_next

    res = right_side * live
    z = factors(res)
    return lax.fori_loop(0, ITERS, body, (jnp.zeros_like(res), res, z, inner(res, z)))[:2]


def call(kernel, outs, scratch=(), smem=1):
    def run(*args):
        return pl.pallas_call(
            kernel,
            out_shape=tuple(jax.ShapeDtypeStruct(shape, f32) for shape in outs),
            in_specs=[SMEM] * smem + [VMEM] * (len(args) - smem),
            out_specs=(VMEM,) * len(outs),
            scratch_shapes=list(scratch),
            compiler_params=pltpu.CompilerParams(vmem_limit_bytes=VMEM_LIMIT),
        )(*args)

    return run


def on_device(
    right_side,
    a_diagonal,
    a_tiles,
    a_columns,
    g_diagonal,
    g_tiles,
    g_columns,
    owned_counts,
    send_lists,
):
    groups, members = lax.axis_size("group"), lax.axis_size("member")
    own = (16, 64, 128)
    message = (4, 64, 128)

    def exchange(msgs):
        out = []
        for c, msg in enumerate(msgs):
            axis, size = (("member", members), ("group", groups))[c // 2]
            if c % 2 == 0:
                pairs = [(i, (((i + 1) ^ 1) - 1) % size) for i in range(size)]
            else:
                pairs = [(i, i ^ 1) for i in range(size)]
            out.append(lax.ppermute(msg, axis, pairs))
        return out

    scratch = [pltpu.VMEM((24, 64, 128), f32), pltpu.VMEM((24, 128, 128), bf16), pltpu.VMEM((24, 64, 128), f32)]
    sizes = (("member", members), ("group", groups))
    msgs = pl.pallas_call(
        functools.partial(pack_kernel, sizes),
        out_shape=(jax.ShapeDtypeStruct((2, 64, 128), f32),) * 4,
        in_specs=[HBM] * 2,
        out_specs=(VMEM,) * 4,
        scratch_shapes=[pltpu.SMEM((1, 4, 2), jnp.int32), pltpu.SemaphoreType.DMA, pltpu.SemaphoreType.DMA((8,))],
        compiler_params=pltpu.CompilerParams(vmem_limit_bytes=VMEM_LIMIT),
    )(send_lists, right_side)
    a_meta, g_meta = pl.pallas_call(
        functools.partial(setup_kernel, sizes),
        out_shape=(jax.ShapeDtypeStruct((97,), jnp.int32), jax.ShapeDtypeStruct((81,), jnp.int32)),
        in_specs=[HBM] * 4,
        out_specs=(SMEM, SMEM),
        scratch_shapes=[
            pltpu.SMEM((16, 5), jnp.int32),
            pltpu.SMEM((16, 4), jnp.int32),
            pltpu.SMEM((1,), jnp.int32),
            pltpu.SMEM((1, 4, 2), jnp.int32),
            pltpu.SemaphoreType.DMA((4,)),
        ],
        compiler_params=pltpu.CompilerParams(vmem_limit_bytes=VMEM_LIMIT),
    )(a_columns, g_columns, owned_counts, send_lists)

    def prepared(tiles):
        count = tiles.shape[1]
        return pl.pallas_call(
            prepare_tiles,
            out_shape=(
                jax.ShapeDtypeStruct((16, count, 128, 256), bf16),
                jax.ShapeDtypeStruct((16, 128 * count, 256), bf16),
            ),
            in_specs=[HBM],
            out_specs=(VMEM, VMEM),
            scratch_shapes=[pltpu.VMEM(tiles.shape, f32), pltpu.SemaphoreType.DMA((16,))],
            compiler_params=pltpu.CompilerParams(vmem_limit_bytes=VMEM_LIMIT),
        )(tiles)

    g_pair, a_pair = prepared(g_tiles), prepared(a_tiles)
    more = [pltpu.VMEM((16, 128, 128), bf16)]
    recvs = exchange(msgs)
    basis_w, basis_v, halves_y = [], [], []
    for k in range(3):
        if k == 0:
            operands = (right_side, *recvs)
        else:
            operands = (part, *msgs, *recvs)
        w, y, part, *msgs = call(functools.partial(factor_kernel, k == 0), [own] * 3 + [message] * 4, scratch + more)(
            g_meta, g_diagonal, *g_pair, *operands
        )
        recvs = exchange(msgs)
        basis_w.append(w)
        halves_y.append(y)
        if k < 2:
            extra = w
            outs = [own, own] + [message] * 4
        else:
            (extra,) = call(gram_kernel, [(64, 128)], smem=0)(*halves_y)
            outs = [own, own] + [(2, 64, 128)] * 4 + [(groups, 8, 128)]
        v, part, *msgs = call(functools.partial(pressure_kernel, k == 2), outs, scratch)(
            a_meta, a_diagonal, *a_pair, part, *msgs, *recvs, extra
        )
        basis_v.append(v)
        if k == 2:
            *msgs, payload = msgs
        recvs = exchange(msgs)
    sums = jnp.sum(lax.all_to_all(payload, "group", 0, 0), axis=0)
    sums = lax.all_to_all(jnp.broadcast_to(sums[None], (members, 8, 128)), "member", 0, 0)
    table, flag = pl.pallas_call(
        scalar_kernel,
        out_shape=(jax.ShapeDtypeStruct((64, 128), f32), jax.ShapeDtypeStruct((1,), jnp.int32)),
        in_specs=[VMEM],
        out_specs=(VMEM, SMEM),
        compiler_params=pltpu.CompilerParams(vmem_limit_bytes=VMEM_LIMIT),
    )(sums)
    inputs = (
        right_side, a_diagonal, a_tiles, a_columns, g_diagonal, g_tiles, g_columns, owned_counts, send_lists
    )
    return lax.cond(
        flag[0] > 0,
        lambda: tuple(plain_steps(*inputs)),
        lambda: tuple(
            call(final_kernel, [own, own], [pltpu.VMEM(own, f32)])(
                a_meta, table, *basis_v, *basis_w, part, *recvs
            )
        ),
    )


def solution(mesh):
    return jax.shard_map(
        on_device,
        mesh=mesh,
        in_specs=(
            P(("group", "member"), None, None),
            P(("group", "member"), None),
            P(("group", "member"), None, None, None),
            P(("group", "member"), None),
            P(("group", "member"), None),
            P(("group", "member"), None, None, None),
            P(("group", "member"), None),
            P(("group", "member")),
            P(("group", "member"), None, None),
        ),
        out_specs=(P(("group", "member"), None, None), P(("group", "member"), None, None)),
        check_vma=False,
    )
```

```python
import functools

import jax
import jax.numpy as jnp
from jax import lax
from jax.experimental import pallas as pl
from jax.experimental.pallas import tpu as pltpu
from jax.sharding import PartitionSpec as P

SHIFT = 4.0
LISTS = 4
VMEM_LIMIT = 10 * 2**20
CANCELLATION = 100.0
ITERS = 3
PRECISE = lax.Precision.HIGHEST
f32 = jnp.float32
bf16 = jnp.bfloat16
VMEM = pl.BlockSpec(memory_space=pltpu.VMEM)
HBM = pl.BlockSpec(memory_space=pltpu.HBM)
SMEM = pl.BlockSpec(memory_space=pltpu.SMEM)


def halves(x):
    high = x.astype(bf16)
    low = (x - high.astype(f32)).astype(bf16)
    return high, low


def stacked(x):
    return jnp.concatenate(halves(x), axis=0)


def beside(x):
    return jnp.concatenate(halves(x), axis=1)


def product(rows, tile):
    out = jnp.dot(rows, tile, preferred_element_type=f32)
    n, m = out.shape[0] // 2, out.shape[1] // 2
    out = out[:n] + out[n:]
    return out[:, :m] + out[:, m:]


class Meta:
    def __init__(self, ref, tiles):
        self.ref = ref
        self.tiles = tiles
        self.base = 16 * tiles

    def column(self, b, k):
        return self.ref[b * self.tiles + k]

    def listed(self, c, s):
        return self.ref[self.base + 2 * c + s]

    def slot(self, c, s):
        return self.ref[self.base + 8 + c] + s

    def valid(self, c):
        return self.ref[self.base + 12 + c] > 0

    def live(self, b):
        return b < self.ref[self.base + 16]


def assemble(meta, part, msgs, recvs, ext):
    for b in range(16):
        ext[b] = part[b]
    for c in range(LISTS):
        valid = meta.valid(c)
        for s in range(2):
            ext[meta.listed(c, s)] += jnp.where(valid, recvs[c][2 + s], 0.0)
            ext[meta.slot(c, s)] = jnp.where(valid, recvs[c][s] + msgs[c][2 + s], 0.0)


def fill_messages(meta, part, sums, sign, msgs):
    for c in range(LISTS):
        for s in range(2):
            msgs[c][s] = part[meta.listed(c, s)]
            msgs[c][2 + s] = sign * sums[meta.slot(c, s)]


def forward_row(meta, b, turned_ref, split_ref):
    picked = [split_ref[meta.column(b, k)] for k in range(meta.tiles)]
    return product(jnp.concatenate(picked, axis=1), turned_ref[b])


def transposed_row(meta, b, near_ref, rows, sums):
    for k in range(meta.tiles):
        sums[meta.column(b, k)] += product(rows, near_ref[b, k])


def prepare_tiles(hbm, near, turned, buffer, sems):
    copies = [pltpu.make_async_copy(hbm.at[b], buffer.at[b], sems.at[b]) for b in range(16)]
    for copy in copies:
        copy.start()
    for b in range(16):
        copies[b].wait()
        for k in range(hbm.shape[1]):
            tile = buffer[b, k]
            near[b, k] = beside(tile)
            turned[b, 128 * k : 128 * (k + 1)] = beside(tile.T)


def ways_of(sizes):
    ways = []
    for axis, size in sizes:
        place = lax.axis_index(axis)
        odd = place % 2
        ways.append((1 - odd, jnp.where(odd == 1, place < size - 1, place > 0)))
        ways.append((odd, jnp.where(odd == 1, place > 0, place < size - 1)))
    return ways


def setup_kernel(sizes, a_hbm, g_hbm, count_hbm, lists_hbm, right_hbm, a_meta, g_meta, m0, m1, m2, m3, *scratch):
    a_cols, g_cols, count, lists, sems, block_sems = scratch
    pairs = ((lists_hbm, lists), (a_hbm, a_cols), (g_hbm, g_cols), (count_hbm, count))
    loads = [pltpu.make_async_copy(source, here, sems.at[i]) for i, (source, here) in enumerate(pairs)]
    for load in loads:
        load.start()
    loads[0].wait()
    ways = ways_of(sizes)
    copies = []
    for c, ((down, _), msg) in enumerate(zip(ways, (m0, m1, m2, m3))):
        for s in range(2):
            row = lists[0, s, 2 * (c // 2) + down]
            copies.append(pltpu.make_async_copy(right_hbm.at[row], msg.at[s], block_sems.at[2 * c + s]))
    for copy in copies:
        copy.start()
    for load in loads[1:]:
        load.wait()
    for cols, meta, tiles in ((a_cols, a_meta, 5), (g_cols, g_meta, 4)):
        base = 16 * tiles
        for b in range(16):
            for k in range(tiles):
                meta[b * tiles + k] = cols[k, b]
        for c, (down, exists) in enumerate(ways):
            first = 2 * (c // 2)
            for s in range(2):
                meta[base + 2 * c + s] = lists[0, s, first + down]
            meta[base + 8 + c] = 16 + 2 * (first + 1 - down)
            meta[base + 12 + c] = exists.astype(jnp.int32)
        meta[base + 16] = count[0]
    for copy in copies:
        copy.wait()


def factor_kernel(first, meta_ref, diag_ref, near_ref, turned_ref, *refs):
    meta = Meta(meta_ref, 4)
    if first:
        right_ref, r0, r1, r2, r3 = refs[:5]
        recvs = (r0, r1, r2, r3)
        own_ref, half_ref, part_ref, m0, m1, m2, m3, ext, split_ref, sums, half_split = refs[5:]
        for b in range(16):
            ext[b] = jnp.where(meta.live(b), right_ref[b], 0.0)
        for c in range(LISTS):
            for s in range(2):
                ext[meta.slot(c, s)] = jnp.where(meta.valid(c), recvs[c][s], 0.0)
    else:
        part_in = refs[0]
        own_ref, half_ref, part_ref, m0, m1, m2, m3, ext, split_ref, sums, half_split = refs[9:]
        assemble(meta, part_in, refs[1:5], refs[5:9], ext)
    for m in range(24):
        split_ref[m] = stacked(ext[m])
    sums[...] = jnp.zeros_like(sums)
    for b in range(16):
        own_ref[b] = ext[b]
    for b in range(16):
        forward = forward_row(meta, b, turned_ref, split_ref)
        half = jnp.where(meta.live(b), diag_ref[b : b + 1] * ext[b] + forward, 0.0)
        half_ref[b] = half
        half_split[b] = stacked(half)
    for b in range(16):
        transposed_row(meta, b, near_ref, half_split[b], sums)
    for b in range(16):
        part_ref[b] = jnp.where(meta.live(b), diag_ref[b : b + 1] * half_ref[b] + sums[b], 0.0)
    fill_messages(meta, part_ref, sums, 1.0, (m0, m1, m2, m3))


def pressure_kernel(last, meta_ref, diag_ref, near_ref, turned_ref, *refs):
    meta = Meta(meta_ref, 5)
    part_in, msgs, recvs = refs[0], refs[1:5], refs[5:9]
    if last:
        gram_ref = refs[9]
        own_ref, part_ref, m0, m1, m2, m3, pay_ref, ext, split_ref, sums = refs[10:]
    else:
        basis_ref = refs[9]
        own_ref, part_ref, m0, m1, m2, m3, ext, split_ref, sums = refs[10:]
    assemble(meta, part_in, msgs, recvs, ext)
    for m in range(24):
        split_ref[m] = stacked(ext[m])
    sums[...] = jnp.zeros_like(sums)
    for b in range(16):
        own_ref[b] = ext[b]
    energy = jnp.zeros(ext.shape[1:], f32)
    for b in range(16):
        forward = forward_row(meta, b, turned_ref, split_ref)
        scaled = diag_ref[b : b + 1] * ext[b]
        part_ref[b] = scaled - forward
        if last:
            energy = energy + ext[b] * (scaled - 2.0 * forward)
        transposed_row(meta, b, near_ref, split_ref[b], sums)
    for b in range(16):
        value = part_ref[b] - sums[b]
        if not last:
            value = value - SHIFT * basis_ref[b]
        part_ref[b] = jnp.where(meta.live(b), value, 0.0)
    if not last:
        fill_messages(meta, part_ref, sums, -1.0, (m0, m1, m2, m3))
    else:
        for c, msg in enumerate((m0, m1, m2, m3)):
            for s in range(2):
                msg[s] = -sums[meta.slot(c, s)]
        place = lax.broadcasted_iota(jnp.int32, energy.shape, 1)
        table = gram_ref[...] + jnp.where(place == 6, jnp.sum(energy, axis=1, keepdims=True), 0.0)
        turned = jnp.concatenate([table, jnp.zeros_like(table)], axis=0).T[:8]
        for i in range(8):
            pay_ref[i] = turned


def gram_kernel(y0, y1, y2, out_ref):
    pairs = ((y0, y0), (y0, y1), (y0, y2), (y1, y1), (y1, y2), (y2, y2))
    totals = [jnp.zeros(out_ref.shape, f32) for _ in pairs]
    for b in range(16):
        totals = [total + left[b] * right[b] for total, (left, right) in zip(totals, pairs)]
    place = lax.broadcasted_iota(jnp.int32, out_ref.shape, 1)
    table = jnp.zeros(out_ref.shape, f32)
    for i, total in enumerate(totals):
        table = table + jnp.where(place == i, jnp.sum(total, axis=1, keepdims=True), 0.0)
    out_ref[...] = table


def cg_scalars(g):
    gram = {(0, 0): g[0], (0, 1): g[1], (0, 2): g[2], (1, 1): g[3], (1, 2): g[4], (2, 2): g[5]}
    size = {at: jnp.abs(value) for at, value in gram.items()}
    energy = {(2, 2): g[6]}
    energy_size = {(2, 2): jnp.abs(g[6])}
    for i in range(2):
        for j in range(i, 3):
            at = (min(i + 1, j), max(i + 1, j))
            energy[i, j] = gram[at] + SHIFT * gram[i, j]
            energy_size[i, j] = size[at] + SHIFT * size[i, j]
    lost = jnp.zeros_like(g[0])

    def form(table, sizes, c, lost):
        total, scale = 0.0, 0.0
        for i in range(len(c)):
            for j in range(i, len(c)):
                pair = c[i] * c[j] * (1.0 if i == j else 2.0)
                total = total + pair * table[i, j]
                scale = scale + jnp.abs(pair) * sizes[i, j]
        return total, jnp.maximum(lost, scale - CANCELLATION * total)

    zero = jnp.zeros_like(g[0])
    one = jnp.ones_like(g[0])
    x = [zero, zero, zero]
    r = [one, zero, zero, zero]
    p = [one]
    rho = gram[0, 0]
    for step in range(ITERS):
        image, lost = form(energy, energy_size, p, lost)
        alpha = rho / image
        for i, c in enumerate(p):
            x[i] = x[i] + alpha * c
            r[i] = r[i] - SHIFT * (alpha * c)
            r[i + 1] = r[i + 1] - alpha * c
        if step + 1 < ITERS:
            rho_next, lost = form(gram, size, r[: step + 2], lost)
            beta = rho_next / rho
            p = [r[i] + beta * (p[i] if i < len(p) else 0.0) for i in range(step + 2)]
            rho = rho_next
    return x + r, lost


def final_kernel(
    meta_ref, sums_ref, v0, v1, v2, w0, w1, w2, part_ref, r0, r1, r2, r3, x_ref, res_ref, flag_ref, w3, table
):
    meta = Meta(meta_ref, 5)
    total = sums_ref[0]
    for i in range(1, sums_ref.shape[0]):
        total = total + sums_ref[i]
    rows, lost = cg_scalars([total[i : i + 1] for i in range(7)])
    lane = lax.broadcasted_iota(jnp.int32, lost.shape, 1)
    bad = jnp.where((lost <= 0.0) | (lane >= 64), 0.0, 1.0)
    flag_ref[0] = (jnp.max(bad) > 0.0).astype(jnp.int32)
    rows = jnp.concatenate(rows + [jnp.zeros((121, 128), f32)], axis=0)
    table[...] = rows.T[:64]
    c = [jnp.broadcast_to(table[:, i : i + 1], (64, 128)) for i in range(7)]
    for b in range(16):
        w3[b] = part_ref[b]
    for i, recv in enumerate((r0, r1, r2, r3)):
        for s in range(2):
            w3[meta.listed(i, s)] += jnp.where(meta.valid(i), recv[s], 0.0)
    for b in range(16):
        x_ref[b] = c[0] * v0[b] + c[1] * v1[b] + c[2] * v2[b]
        res_ref[b] = c[3] * w0[b] + c[4] * w1[b] + (c[5] - SHIFT * c[6]) * w2[b] + c[6] * w3[b]


def plain_steps(
    right_side, a_diagonal, a_tiles, a_columns, g_diagonal, g_tiles, g_columns, owned_counts, send_lists
):
    outgoing = send_lists[0]
    live = (jnp.arange(16) < owned_counts[0]).astype(f32)[:, None, None]
    a_scale, g_scale = a_diagonal[:, None, :], g_diagonal[:, None, :]
    steps = (("member", 1), ("member", -1), ("group", 1), ("group", -1))

    def move(block, axis, way):
        size = lax.axis_size(axis)
        return lax.ppermute(block, axis, [(i, i + way) for i in range(size) if 0 <= i + way < size])

    def forward(tiles, columns, vector):
        halo = [move(vector[outgoing[j]], axis, way) for j, (axis, way) in enumerate(steps)]
        picked = jnp.concatenate([vector] + halo, axis=0)[columns]
        return jnp.einsum("rkij,rknj->rni", tiles, picked, precision=PRECISE)

    def backward(tiles, columns, vector):
        parts = jnp.einsum("rkij,rni->rknj", tiles, vector, precision=PRECISE)
        onehot = (columns.reshape(-1)[:, None] == jnp.arange(24)[None, :]).astype(f32)
        wide = jnp.einsum("te,tnb->enb", onehot, parts.reshape((-1,) + vector.shape[1:]), precision=PRECISE)
        back = [move(wide[16 + 2 * j : 18 + 2 * j], axis, -way) for j, (axis, way) in enumerate(steps)]
        places = (outgoing.reshape(-1)[:, None] == jnp.arange(16)[None, :]).astype(f32)
        return wide[:16] + jnp.einsum("sr,snb->rnb", places, jnp.concatenate(back, axis=0), precision=PRECISE)

    def factors(vector):
        half = (g_scale * vector + forward(g_tiles, g_columns, vector)) * live
        return (g_scale * half + backward(g_tiles, g_columns, half)) * live

    def inner(u, w):
        own = jnp.zeros((8, 128), f32).at[0, :64].set(jnp.sum(u * w, axis=(0, 2)))
        for axis in ("group", "member"):
            spread = jnp.broadcast_to(own[None], (lax.axis_size(axis), 8, 128))
            own = jnp.sum(lax.all_to_all(spread, axis, 0, 0), axis=0)
        return own[0, :64]

    def body(step, carry):
        x, res, direction, rho = carry
        z = factors(res)
        rho_next = inner(res, z)
        direction = z + jnp.where(step == 0, 0.0, rho_next / rho)[:, None] * direction
        low = forward(a_tiles, a_columns, direction)
        image = (a_scale * direction - low - backward(a_tiles, a_columns, direction)) * live
        alpha = (rho_next / inner(direction, image))[:, None]
        return x + alpha * direction, res - alpha * image, direction, rho_next

    res = right_side * live
    zero = jnp.zeros_like(res)
    return lax.fori_loop(0, ITERS, body, (zero, res, zero, jnp.ones((64,), f32)))[:2]


def call(kernel, outs, scratch=(), smem=1):
    def run(*args):
        return pl.pallas_call(
            kernel,
            out_shape=tuple(jax.ShapeDtypeStruct(shape, f32) for shape in outs),
            in_specs=[SMEM] * smem + [VMEM] * (len(args) - smem),
            out_specs=(VMEM,) * len(outs),
            scratch_shapes=list(scratch),
            compiler_params=pltpu.CompilerParams(vmem_limit_bytes=VMEM_LIMIT),
        )(*args)

    return run


def on_device(
    right_side,
    a_diagonal,
    a_tiles,
    a_columns,
    g_diagonal,
    g_tiles,
    g_columns,
    owned_counts,
    send_lists,
):
    groups, members = lax.axis_size("group"), lax.axis_size("member")
    own = (16, 64, 128)
    message = (4, 64, 128)

    def exchange(msgs):
        out = []
        for c, msg in enumerate(msgs):
            axis, size = (("member", members), ("group", groups))[c // 2]
            if c % 2 == 0:
                pairs = [(i, (((i + 1) ^ 1) - 1) % size) for i in range(size)]
            else:
                pairs = [(i, i ^ 1) for i in range(size)]
            out.append(lax.ppermute(msg, axis, pairs))
        return out

    scratch = [pltpu.VMEM((24, 64, 128), f32), pltpu.VMEM((24, 128, 128), bf16), pltpu.VMEM((24, 64, 128), f32)]
    sizes = (("member", members), ("group", groups))
    a_meta, g_meta, *msgs = pl.pallas_call(
        functools.partial(setup_kernel, sizes),
        out_shape=(jax.ShapeDtypeStruct((97,), jnp.int32), jax.ShapeDtypeStruct((81,), jnp.int32))
        + (jax.ShapeDtypeStruct((2, 64, 128), f32),) * 4,
        in_specs=[HBM] * 5,
        out_specs=(SMEM, SMEM) + (VMEM,) * 4,
        scratch_shapes=[
            pltpu.SMEM((5, 16), jnp.int32),
            pltpu.SMEM((4, 16), jnp.int32),
            pltpu.SMEM((1,), jnp.int32),
            pltpu.SMEM((1, 2, 4), jnp.int32),
            pltpu.SemaphoreType.DMA((4,)),
            pltpu.SemaphoreType.DMA((8,)),
        ],
        compiler_params=pltpu.CompilerParams(vmem_limit_bytes=VMEM_LIMIT),
    )(a_columns.T, g_columns.T, owned_counts, jnp.transpose(send_lists, (0, 2, 1)), right_side)

    def prepared(tiles):
        count = tiles.shape[1]
        return pl.pallas_call(
            prepare_tiles,
            out_shape=(
                jax.ShapeDtypeStruct((16, count, 128, 256), bf16),
                jax.ShapeDtypeStruct((16, 128 * count, 256), bf16),
            ),
            in_specs=[HBM],
            out_specs=(VMEM, VMEM),
            scratch_shapes=[pltpu.VMEM(tiles.shape, f32), pltpu.SemaphoreType.DMA((16,))],
            compiler_params=pltpu.CompilerParams(vmem_limit_bytes=VMEM_LIMIT),
        )(tiles)

    g_pair, a_pair = prepared(g_tiles), prepared(a_tiles)
    more = [pltpu.VMEM((16, 128, 128), bf16)]
    recvs = exchange(msgs)
    basis_w, basis_v, halves_y = [], [], []
    for k in range(3):
        if k == 0:
            operands = (right_side, *recvs)
        else:
            operands = (part, *msgs, *recvs)
        w, y, part, *msgs = call(functools.partial(factor_kernel, k == 0), [own] * 3 + [message] * 4, scratch + more)(
            g_meta, g_diagonal, *g_pair, *operands
        )
        recvs = exchange(msgs)
        basis_w.append(w)
        halves_y.append(y)
        if k < 2:
            extra = w
            outs = [own, own] + [message] * 4
        else:
            (extra,) = call(gram_kernel, [(64, 128)], smem=0)(*halves_y)
            outs = [own, own] + [(2, 64, 128)] * 4 + [(groups, 8, 128)]
        v, part, *msgs = call(functools.partial(pressure_kernel, k == 2), outs, scratch)(
            a_meta, a_diagonal, *a_pair, part, *msgs, *recvs, extra
        )
        basis_v.append(v)
        if k == 2:
            *msgs, payload = msgs
        recvs = exchange(msgs)
    sums = jnp.sum(lax.all_to_all(payload, "group", 0, 0), axis=0)
    sums = lax.all_to_all(jnp.broadcast_to(sums[None], (members, 8, 128)), "member", 0, 0)
    x, res, flag = pl.pallas_call(
        final_kernel,
        out_shape=(jax.ShapeDtypeStruct(own, f32),) * 2 + (jax.ShapeDtypeStruct((1,), jnp.int32),),
        in_specs=[SMEM] + [VMEM] * 12,
        out_specs=(VMEM, VMEM, SMEM),
        scratch_shapes=[pltpu.VMEM(own, f32), pltpu.VMEM((64, 128), f32)],
        compiler_params=pltpu.CompilerParams(vmem_limit_bytes=VMEM_LIMIT),
    )(a_meta, sums, *basis_v, *basis_w, part, *recvs)
    inputs = (
        right_side, a_diagonal, a_tiles, a_columns, g_diagonal, g_tiles, g_columns, owned_counts, send_lists
    )
    _, x, res = lax.while_loop(
        lambda carry: carry[0] > 0, lambda carry: (jnp.int32(0), *plain_steps(*inputs)), (flag[0], x, res)
    )
    return x, res


def solution(mesh):
    return jax.shard_map(
        on_device,
        mesh=mesh,
        in_specs=(
            P(("group", "member"), None, None),
            P(("group", "member"), None),
            P(("group", "member"), None, None, None),
            P(("group", "member"), None),
            P(("group", "member"), None),
            P(("group", "member"), None, None, None),
            P(("group", "member"), None),
            P(("group", "member")),
            P(("group", "member"), None, None),
        ),
        out_specs=(P(("group", "member"), None, None), P(("group", "member"), None, None)),
        check_vma=False,
    )
```

```python
import functools

import jax
import jax.numpy as jnp
from jax import lax
from jax.experimental import pallas as pl
from jax.experimental.pallas import tpu as pltpu
from jax.sharding import PartitionSpec as P

SHIFT = 4.0
LISTS = 4
VMEM_LIMIT = 10 * 2**20
CANCELLATION = 100.0
ITERS = 3
PRECISE = lax.Precision.HIGHEST
f32 = jnp.float32
bf16 = jnp.bfloat16
VMEM = pl.BlockSpec(memory_space=pltpu.VMEM)
HBM = pl.BlockSpec(memory_space=pltpu.HBM)
SMEM = pl.BlockSpec(memory_space=pltpu.SMEM)


def halves(x):
    high = x.astype(bf16)
    low = (x - high.astype(f32)).astype(bf16)
    return high, low


def stacked(x):
    return jnp.concatenate(halves(x), axis=0)


def beside(x):
    return jnp.concatenate(halves(x), axis=1)


def product(rows, tile):
    out = jnp.dot(rows, tile, preferred_element_type=f32)
    n, m = out.shape[0] // 2, out.shape[1] // 2
    out = out[:n] + out[n:]
    return out[:, :m] + out[:, m:]


class Meta:
    def __init__(self, ref, tiles):
        self.ref = ref
        self.tiles = tiles
        self.base = 16 * tiles

    def column(self, b, k):
        return self.ref[b * self.tiles + k]

    def listed(self, c, s):
        return self.ref[self.base + 2 * c + s]

    def slot(self, c, s):
        return self.ref[self.base + 8 + c] + s

    def valid(self, c):
        return self.ref[self.base + 12 + c] > 0

    def live(self, b):
        return b < self.ref[self.base + 16]


def assemble(meta, part, msgs, recvs, ext):
    for b in range(16):
        ext[b] = part[b]
    for c in range(LISTS):
        valid = meta.valid(c)
        for s in range(2):
            ext[meta.listed(c, s)] += jnp.where(valid, recvs[c][2 + s], 0.0)
            ext[meta.slot(c, s)] = jnp.where(valid, recvs[c][s] + msgs[c][2 + s], 0.0)


def fill_messages(meta, part, sums, sign, msgs):
    for c in range(LISTS):
        for s in range(2):
            msgs[c][s] = part[meta.listed(c, s)]
            msgs[c][2 + s] = sign * sums[meta.slot(c, s)]


def forward_row(meta, b, turned_ref, split_ref):
    picked = [split_ref[meta.column(b, k)] for k in range(meta.tiles)]
    return product(jnp.concatenate(picked, axis=1), turned_ref[b])


def transposed_row(meta, b, near_ref, rows, sums):
    for k in range(meta.tiles):
        sums[meta.column(b, k)] += product(rows, near_ref[b, k])


def prepare_tiles(hbm, near, turned, buffer, sems):
    copies = [pltpu.make_async_copy(hbm.at[b], buffer.at[b], sems.at[b]) for b in range(16)]
    for copy in copies:
        copy.start()
    for b in range(16):
        copies[b].wait()
        for k in range(hbm.shape[1]):
            tile = buffer[b, k]
            near[b, k] = beside(tile)
            turned[b, 128 * k : 128 * (k + 1)] = beside(tile.T)


def ways_of(sizes):
    ways = []
    for axis, size in sizes:
        place = lax.axis_index(axis)
        odd = place % 2
        ways.append((1 - odd, jnp.where(odd == 1, place < size - 1, place > 0)))
        ways.append((odd, jnp.where(odd == 1, place > 0, place < size - 1)))
    return ways


def setup_kernel(sizes, a_hbm, g_hbm, count_hbm, lists_hbm, right_hbm, a_meta, g_meta, m0, m1, m2, m3, *scratch):
    a_cols, g_cols, count, lists, sems, block_sems = scratch
    pairs = ((lists_hbm, lists), (a_hbm, a_cols), (g_hbm, g_cols), (count_hbm, count))
    loads = [pltpu.make_async_copy(source, here, sems.at[i]) for i, (source, here) in enumerate(pairs)]
    for load in loads:
        load.start()
    loads[0].wait()
    ways = ways_of(sizes)
    copies = []
    for c, ((down, _), msg) in enumerate(zip(ways, (m0, m1, m2, m3))):
        for s in range(2):
            row = lists[0, s, 2 * (c // 2) + down]
            copies.append(pltpu.make_async_copy(right_hbm.at[row], msg.at[s], block_sems.at[2 * c + s]))
    for copy in copies:
        copy.start()
    for load in loads[1:]:
        load.wait()
    for cols, meta, tiles in ((a_cols, a_meta, 5), (g_cols, g_meta, 4)):
        base = 16 * tiles
        for b in range(16):
            for k in range(tiles):
                meta[b * tiles + k] = cols[k, b]
        for c, (down, exists) in enumerate(ways):
            first = 2 * (c // 2)
            for s in range(2):
                meta[base + 2 * c + s] = lists[0, s, first + down]
            meta[base + 8 + c] = 16 + 2 * (first + 1 - down)
            meta[base + 12 + c] = exists.astype(jnp.int32)
        meta[base + 16] = count[0]
    for copy in copies:
        copy.wait()


def factor_kernel(first, meta_ref, diag_ref, near_ref, turned_ref, *refs):
    meta = Meta(meta_ref, 4)
    if first:
        right_ref, r0, r1, r2, r3 = refs[:5]
        recvs = (r0, r1, r2, r3)
        own_ref, half_ref, part_ref, m0, m1, m2, m3, ext, split_ref, sums, half_split = refs[5:]
        for b in range(16):
            ext[b] = jnp.where(meta.live(b), right_ref[b], 0.0)
        for c in range(LISTS):
            for s in range(2):
                ext[meta.slot(c, s)] = jnp.where(meta.valid(c), recvs[c][s], 0.0)
    else:
        part_in = refs[0]
        own_ref, half_ref, part_ref, m0, m1, m2, m3, ext, split_ref, sums, half_split = refs[9:]
        assemble(meta, part_in, refs[1:5], refs[5:9], ext)
    for m in range(24):
        split_ref[m] = stacked(ext[m])
    sums[...] = jnp.zeros_like(sums)
    for b in range(16):
        own_ref[b] = ext[b]
    for b in range(16):
        forward = forward_row(meta, b, turned_ref, split_ref)
        half = jnp.where(meta.live(b), diag_ref[b : b + 1] * ext[b] + forward, 0.0)
        half_ref[b] = half
        half_split[b] = stacked(half)
    for b in range(16):
        transposed_row(meta, b, near_ref, half_split[b], sums)
    for b in range(16):
        part_ref[b] = jnp.where(meta.live(b), diag_ref[b : b + 1] * half_ref[b] + sums[b], 0.0)
    fill_messages(meta, part_ref, sums, 1.0, (m0, m1, m2, m3))


def pressure_kernel(last, meta_ref, diag_ref, tile_ref, *refs):
    meta = Meta(meta_ref, 5)
    part_in, msgs, recvs = refs[0], refs[1:5], refs[5:9]
    if last:
        gram_ref = refs[9]
        own_ref, part_ref, m0, m1, m2, m3, pay_ref, ext, split_ref, sums = refs[10:]
    else:
        basis_ref = refs[9]
        own_ref, part_ref, m0, m1, m2, m3, ext, split_ref, sums = refs[10:]
    assemble(meta, part_in, msgs, recvs, ext)
    for m in range(24):
        split_ref[m] = stacked(ext[m])
    sums[...] = jnp.zeros_like(sums)
    for b in range(16):
        own_ref[b] = ext[b]
    energy = jnp.zeros(ext.shape[1:], f32)
    for b in range(16):
        picked = [split_ref[meta.column(b, k)] for k in range(5)]
        turned = [beside(tile_ref[b, k].T) for k in range(5)]
        forward = product(jnp.concatenate(picked, axis=1), jnp.concatenate(turned, axis=0))
        scaled = diag_ref[b : b + 1] * ext[b]
        part_ref[b] = scaled - forward
        if last:
            energy = energy + ext[b] * (scaled - 2.0 * forward)
        for k in range(5):
            sums[meta.column(b, k)] += product(split_ref[b], beside(tile_ref[b, k]))
    for b in range(16):
        value = part_ref[b] - sums[b]
        if not last:
            value = value - SHIFT * basis_ref[b]
        part_ref[b] = jnp.where(meta.live(b), value, 0.0)
    if not last:
        fill_messages(meta, part_ref, sums, -1.0, (m0, m1, m2, m3))
    else:
        for c, msg in enumerate((m0, m1, m2, m3)):
            for s in range(2):
                msg[s] = -sums[meta.slot(c, s)]
        place = lax.broadcasted_iota(jnp.int32, energy.shape, 1)
        table = gram_ref[...] + jnp.where(place == 6, jnp.sum(energy, axis=1, keepdims=True), 0.0)
        turned = jnp.concatenate([table, jnp.zeros_like(table)], axis=0).T[:8]
        for i in range(8):
            pay_ref[i] = turned


def gram_kernel(y0, y1, y2, out_ref):
    pairs = ((y0, y0), (y0, y1), (y0, y2), (y1, y1), (y1, y2), (y2, y2))
    totals = [jnp.zeros(out_ref.shape, f32) for _ in pairs]
    for b in range(16):
        totals = [total + left[b] * right[b] for total, (left, right) in zip(totals, pairs)]
    place = lax.broadcasted_iota(jnp.int32, out_ref.shape, 1)
    table = jnp.zeros(out_ref.shape, f32)
    for i, total in enumerate(totals):
        table = table + jnp.where(place == i, jnp.sum(total, axis=1, keepdims=True), 0.0)
    out_ref[...] = table


def cg_scalars(g):
    gram = {(0, 0): g[0], (0, 1): g[1], (0, 2): g[2], (1, 1): g[3], (1, 2): g[4], (2, 2): g[5]}
    size = {at: jnp.abs(value) for at, value in gram.items()}
    energy = {(2, 2): g[6]}
    energy_size = {(2, 2): jnp.abs(g[6])}
    for i in range(2):
        for j in range(i, 3):
            at = (min(i + 1, j), max(i + 1, j))
            energy[i, j] = gram[at] + SHIFT * gram[i, j]
            energy_size[i, j] = size[at] + SHIFT * size[i, j]
    lost = jnp.zeros_like(g[0])

    def form(table, sizes, c, lost):
        total, scale = 0.0, 0.0
        for i in range(len(c)):
            for j in range(i, len(c)):
                pair = c[i] * c[j] * (1.0 if i == j else 2.0)
                total = total + pair * table[i, j]
                scale = scale + jnp.abs(pair) * sizes[i, j]
        return total, jnp.maximum(lost, scale - CANCELLATION * total)

    zero = jnp.zeros_like(g[0])
    one = jnp.ones_like(g[0])
    x = [zero, zero, zero]
    r = [one, zero, zero, zero]
    p = [one]
    rho = gram[0, 0]
    for step in range(ITERS):
        image, lost = form(energy, energy_size, p, lost)
        alpha = rho / image
        for i, c in enumerate(p):
            x[i] = x[i] + alpha * c
            r[i] = r[i] - SHIFT * (alpha * c)
            r[i + 1] = r[i + 1] - alpha * c
        if step + 1 < ITERS:
            rho_next, lost = form(gram, size, r[: step + 2], lost)
            beta = rho_next / rho
            p = [r[i] + beta * (p[i] if i < len(p) else 0.0) for i in range(step + 2)]
            rho = rho_next
    return x + r, lost


def final_kernel(
    meta_ref, sums_ref, v0, v1, v2, w0, w1, w2, part_ref, r0, r1, r2, r3, x_ref, res_ref, flag_ref, w3, table
):
    meta = Meta(meta_ref, 5)
    total = sums_ref[0]
    for i in range(1, sums_ref.shape[0]):
        total = total + sums_ref[i]
    rows, lost = cg_scalars([total[i : i + 1] for i in range(7)])
    lane = lax.broadcasted_iota(jnp.int32, lost.shape, 1)
    bad = jnp.where((lost <= 0.0) | (lane >= 64), 0.0, 1.0)
    flag_ref[0] = (jnp.max(bad) > 0.0).astype(jnp.int32)
    rows = jnp.concatenate(rows + [jnp.zeros((121, 128), f32)], axis=0)
    table[...] = rows.T[:64]
    c = [jnp.broadcast_to(table[:, i : i + 1], (64, 128)) for i in range(7)]
    for b in range(16):
        w3[b] = part_ref[b]
    for i, recv in enumerate((r0, r1, r2, r3)):
        for s in range(2):
            w3[meta.listed(i, s)] += jnp.where(meta.valid(i), recv[s], 0.0)
    for b in range(16):
        x_ref[b] = c[0] * v0[b] + c[1] * v1[b] + c[2] * v2[b]
        res_ref[b] = c[3] * w0[b] + c[4] * w1[b] + (c[5] - SHIFT * c[6]) * w2[b] + c[6] * w3[b]


def plain_steps(
    right_side, a_diagonal, a_tiles, a_columns, g_diagonal, g_tiles, g_columns, owned_counts, send_lists
):
    outgoing = send_lists[0]
    live = (jnp.arange(16) < owned_counts[0]).astype(f32)[:, None, None]
    a_scale, g_scale = a_diagonal[:, None, :], g_diagonal[:, None, :]
    steps = (("member", 1), ("member", -1), ("group", 1), ("group", -1))

    def move(block, axis, way):
        size = lax.axis_size(axis)
        return lax.ppermute(block, axis, [(i, i + way) for i in range(size) if 0 <= i + way < size])

    def forward(tiles, columns, vector):
        halo = [move(vector[outgoing[j]], axis, way) for j, (axis, way) in enumerate(steps)]
        extended = jnp.concatenate([vector] + halo, axis=0)

        def add(at, total):
            b, k = at // tiles.shape[1], at % tiles.shape[1]
            term = jnp.dot(extended[columns[b, k]], tiles[b, k].T, precision=PRECISE)
            return total.at[b].add(term)

        return lax.fori_loop(0, 16 * tiles.shape[1], add, jnp.zeros_like(vector))

    def backward(tiles, columns, vector):
        def add(at, total):
            b, k = at // tiles.shape[1], at % tiles.shape[1]
            return total.at[columns[b, k]].add(jnp.dot(vector[b], tiles[b, k], precision=PRECISE))

        wide = lax.fori_loop(0, 16 * tiles.shape[1], add, jnp.zeros((24,) + vector.shape[1:], f32))
        back = [move(wide[16 + 2 * j : 18 + 2 * j], axis, -way) for j, (axis, way) in enumerate(steps)]
        back = jnp.concatenate(back, axis=0)
        return lax.fori_loop(
            0, 8, lambda at, total: total.at[outgoing[at // 2, at % 2]].add(back[at]), wide[:16]
        )

    def factors(vector):
        half = (g_scale * vector + forward(g_tiles, g_columns, vector)) * live
        return (g_scale * half + backward(g_tiles, g_columns, half)) * live

    def inner(u, w):
        own = jnp.zeros((8, 128), f32).at[0, :64].set(jnp.sum(u * w, axis=(0, 2)))
        for axis in ("group", "member"):
            spread = jnp.broadcast_to(own[None], (lax.axis_size(axis), 8, 128))
            own = jnp.sum(lax.all_to_all(spread, axis, 0, 0), axis=0)
        return own[0, :64]

    def body(step, carry):
        x, res, direction, rho = carry
        z = factors(res)
        rho_next = inner(res, z)
        direction = z + jnp.where(step == 0, 0.0, rho_next / rho)[:, None] * direction
        low = forward(a_tiles, a_columns, direction)
        image = (a_scale * direction - low - backward(a_tiles, a_columns, direction)) * live
        alpha = (rho_next / inner(direction, image))[:, None]
        return x + alpha * direction, res - alpha * image, direction, rho_next

    res = right_side * live
    zero = jnp.zeros_like(res)
    return lax.fori_loop(0, ITERS, body, (zero, res, zero, jnp.ones((64,), f32)))[:2]


def call(kernel, outs, scratch=(), smem=1):
    def run(*args):
        return pl.pallas_call(
            kernel,
            out_shape=tuple(jax.ShapeDtypeStruct(shape, f32) for shape in outs),
            in_specs=[SMEM] * smem + [VMEM] * (len(args) - smem),
            out_specs=(VMEM,) * len(outs),
            scratch_shapes=list(scratch),
            compiler_params=pltpu.CompilerParams(vmem_limit_bytes=VMEM_LIMIT),
        )(*args)

    return run


def on_device(
    right_side,
    a_diagonal,
    a_tiles,
    a_columns,
    g_diagonal,
    g_tiles,
    g_columns,
    owned_counts,
    send_lists,
):
    groups, members = lax.axis_size("group"), lax.axis_size("member")
    own = (16, 64, 128)
    message = (4, 64, 128)

    def exchange(msgs):
        out = []
        for c, msg in enumerate(msgs):
            axis, size = (("member", members), ("group", groups))[c // 2]
            if c % 2 == 0:
                pairs = [(i, (((i + 1) ^ 1) - 1) % size) for i in range(size)]
            else:
                pairs = [(i, i ^ 1) for i in range(size)]
            out.append(lax.ppermute(msg, axis, pairs))
        return out

    scratch = [pltpu.VMEM((24, 64, 128), f32), pltpu.VMEM((24, 128, 128), bf16), pltpu.VMEM((24, 64, 128), f32)]
    sizes = (("member", members), ("group", groups))
    a_meta, g_meta, *msgs = pl.pallas_call(
        functools.partial(setup_kernel, sizes),
        out_shape=(jax.ShapeDtypeStruct((97,), jnp.int32), jax.ShapeDtypeStruct((81,), jnp.int32))
        + (jax.ShapeDtypeStruct((2, 64, 128), f32),) * 4,
        in_specs=[HBM] * 5,
        out_specs=(SMEM, SMEM) + (VMEM,) * 4,
        scratch_shapes=[
            pltpu.SMEM((5, 16), jnp.int32),
            pltpu.SMEM((4, 16), jnp.int32),
            pltpu.SMEM((1,), jnp.int32),
            pltpu.SMEM((1, 2, 4), jnp.int32),
            pltpu.SemaphoreType.DMA((4,)),
            pltpu.SemaphoreType.DMA((8,)),
        ],
        compiler_params=pltpu.CompilerParams(vmem_limit_bytes=VMEM_LIMIT),
    )(a_columns.T, g_columns.T, owned_counts, jnp.transpose(send_lists, (0, 2, 1)), right_side)

    def prepared(tiles):
        count = tiles.shape[1]
        return pl.pallas_call(
            prepare_tiles,
            out_shape=(
                jax.ShapeDtypeStruct((16, count, 128, 256), bf16),
                jax.ShapeDtypeStruct((16, 128 * count, 256), bf16),
            ),
            in_specs=[HBM],
            out_specs=(VMEM, VMEM),
            scratch_shapes=[pltpu.VMEM(tiles.shape, f32), pltpu.SemaphoreType.DMA((16,))],
            compiler_params=pltpu.CompilerParams(vmem_limit_bytes=VMEM_LIMIT),
        )(tiles)

    g_pair = prepared(g_tiles)
    more = [pltpu.VMEM((16, 128, 128), bf16)]
    recvs = exchange(msgs)
    basis_w, basis_v, halves_y = [], [], []
    for k in range(3):
        if k == 0:
            operands = (right_side, *recvs)
        else:
            operands = (part, *msgs, *recvs)
        w, y, part, *msgs = call(functools.partial(factor_kernel, k == 0), [own] * 3 + [message] * 4, scratch + more)(
            g_meta, g_diagonal, *g_pair, *operands
        )
        recvs = exchange(msgs)
        basis_w.append(w)
        halves_y.append(y)
        if k < 2:
            extra = w
            outs = [own, own] + [message] * 4
        else:
            (extra,) = call(gram_kernel, [(64, 128)], smem=0)(*halves_y)
            outs = [own, own] + [(2, 64, 128)] * 4 + [(groups, 8, 128)]
        v, part, *msgs = call(functools.partial(pressure_kernel, k == 2), outs, scratch)(
            a_meta, a_diagonal, a_tiles, part, *msgs, *recvs, extra
        )
        basis_v.append(v)
        if k == 2:
            *msgs, payload = msgs
        recvs = exchange(msgs)
    sums = jnp.sum(lax.all_to_all(payload, "group", 0, 0), axis=0)
    sums = lax.all_to_all(jnp.broadcast_to(sums[None], (members, 8, 128)), "member", 0, 0)
    x, res, flag = pl.pallas_call(
        final_kernel,
        out_shape=(jax.ShapeDtypeStruct(own, f32),) * 2 + (jax.ShapeDtypeStruct((1,), jnp.int32),),
        in_specs=[SMEM] + [VMEM] * 12,
        out_specs=(VMEM, VMEM, SMEM),
        scratch_shapes=[pltpu.VMEM(own, f32), pltpu.VMEM((64, 128), f32)],
        compiler_params=pltpu.CompilerParams(vmem_limit_bytes=VMEM_LIMIT),
    )(a_meta, sums, *basis_v, *basis_w, part, *recvs)
    inputs = (
        right_side, a_diagonal, a_tiles, a_columns, g_diagonal, g_tiles, g_columns, owned_counts, send_lists
    )
    _, x, res = lax.while_loop(
        lambda carry: carry[0] > 0, lambda carry: (jnp.int32(0), *plain_steps(*inputs)), (flag[0], x, res)
    )
    return x, res


def solution(mesh):
    return jax.shard_map(
        on_device,
        mesh=mesh,
        in_specs=(
            P(("group", "member"), None, None),
            P(("group", "member"), None),
            P(("group", "member"), None, None, None),
            P(("group", "member"), None),
            P(("group", "member"), None),
            P(("group", "member"), None, None, None),
            P(("group", "member"), None),
            P(("group", "member")),
            P(("group", "member"), None, None),
        ),
        out_specs=(P(("group", "member"), None, None), P(("group", "member"), None, None)),
        check_vma=False,
    )
```
